32 devices in a mesh: dp: 4 (over y, x), rows: 8 (over z, core).
Axes of the slice: x: 2, y: 2, z: 4, core: 2. Of those that a mesh axis runs over, the one named last changes fastest.
Arguments:
- inputs: bfloat16 [4, 512, 64, 384], P('dp', 'rows'), may hold values from -6 to 6
- cotangent: bfloat16 [4, 512, 64, 384], P('dp', 'rows'), may hold values from -6 to 6
- weight_one: bfloat16 [3456, 384], replicated, may hold values from -0.109375 to 0.109375
- weight_two: bfloat16 [3456, 384], replicated, may hold values from -0.109375 to 0.109375
Outputs:
- output: bfloat16 [4, 512, 64, 384], P('dp', 'rows')
- grad_one: float32 [3456, 384], P('rows', 'dp')
- grad_two: float32 [3456, 384], P('rows', 'dp')
The draws below stay inside these ranges and needn't reach their ends.
All inputs are finite; a program needn't handle non-finite values.
Results may differ from the reference program's by a relative error of at most 0.006.
Values may be sent and summed in bfloat16 or wider, within the bound.
A program may use at most 192 MiB of HBM per device.

```python
import math
import jax
import jax.numpy as jnp
from jax import lax

C = 384
H = 512
COLS = 64
DILATION_STEP = 16
SAMPLES = 4


def strengthened(entries, own_key, source, target, shards_of, factor):
    owner, partner = [(jnp.arange(entries.shape[dim]) // (entries.shape[dim] // shards_of)).reshape([-1 if axis == dim else 1 for axis in range(entries.ndim)]) for dim in (source, target)]
    chosen = jax.random.permutation(own_key, shards_of)[partner]
    strong = (owner == chosen) | (owner == (partner + shards_of // 2) % shards_of)
    return jnp.where(strong, factor * entries, entries)


def block_scale(own_key, shape, shards, low, top_value):
    factor_of, own = 1.0, jax.random.fold_in(own_key, 6)
    for position, parts in shards:
        steps = jnp.exp(jax.random.uniform(jax.random.fold_in(own, position), (parts,), jnp.float32, low / len(shards), top_value / len(shards)))
        factor_of = factor_of * jnp.repeat(steps, shape[position] // parts).reshape([-1 if axis == position else 1 for axis in range(len(shape))])
    return factor_of


def bell_draw(rng, shape, deviation, reach, cuts=(), kind=jnp.bfloat16):
    array = jax.random.normal(rng, shape, jnp.float32) * deviation
    if len(cuts) > 0:
        array = block_scale(rng, shape, cuts, -0.22, 0.18) * array
    return jnp.clip(array, min=-reach, max=reach).astype(kind)


def noise_with(rng, shape, deviation, most, shards, heavy, held_as=jnp.bfloat16):
    values = deviation * jax.random.normal(rng, shape, jnp.float32)
    if shards:
        values = values * block_scale(rng, shape, shards, -0.22, 0.18)
    return jnp.clip(strengthened(values, jax.random.fold_in(rng, 3), *heavy), -most, most).astype(held_as)


def setup_inputs(seed: int = 0) -> dict:
    streams_of = jax.random.split(jax.random.key(seed), 5)
    inputs = bell_draw(streams_of[0], (SAMPLES, H, COLS, C), 1.0, 6.0, ((0, 4), (1, 8)))
    cotangent = noise_with(streams_of[1], (SAMPLES, H, COLS, C), 1.0, 6.0, ((0, 4), (1, 8)), (0, 3, 4, 2.0))
    weight_one = bell_draw(streams_of[2], (9 * C, C), (9 * C) ** -0.5, 0.109375)
    weight_two = bell_draw(streams_of[3], (9 * C, C), (9 * C) ** -0.5, 0.109375)
    return dict(inputs=inputs, cotangent=cotangent, weight_one=weight_one, weight_two=weight_two)


def stack_taps(padded, count_rows, count_cols, pad_rows, pad_cols, step_rows, step_cols, direction):
    pieces = []
    for offset_row in (-1, 0, 1):
        for offset_col in (-1, 0, 1):
            first_row = pad_rows + direction * offset_row * step_rows
            first_col = pad_cols + direction * offset_col * step_cols
            pieces.append(padded[first_row:first_row + count_rows, first_col:first_col + count_cols, :])
    return jnp.concatenate(pieces, axis=-1)

def dilated_convolution(image, spacing, direction):
    padded = jnp.pad(image, ((spacing, spacing), (spacing, spacing), (0, 0)))
    return stack_taps(padded, image.shape[0], image.shape[1], spacing, spacing, spacing, spacing, direction)

def flipped(weights):
    channel_count = weights.shape[1]
    return jnp.transpose(weights.reshape(9, channel_count, channel_count), (0, 2, 1)).reshape(9 * channel_count, channel_count)

def contract(stacked, target):
    return lax.dot_general(stacked, target, (((0,), (0,)), ((), ())), preferred_element_type=jnp.float32)

def reference(inputs, cotangent, weight_one, weight_two):
    samples, height, width, channel_count = inputs.shape
    rotated_kernel = flipped(weight_two)

    def one_sample(pair):
        image, upstream_gradient = pair
        near = dilated_convolution(image, 4, 1).reshape(-1, 9 * channel_count)
        before = jnp.dot(near, weight_one, preferred_element_type=jnp.float32)
        hidden_state = jnp.maximum(before, 0.0).astype(jnp.bfloat16).reshape(height, width, channel_count)
        distant_frame = dilated_convolution(hidden_state, DILATION_STEP, 1).reshape(-1, 9 * channel_count)
        result = jnp.dot(distant_frame, weight_two, preferred_element_type=jnp.float32).astype(jnp.bfloat16)
        grad_two = contract(distant_frame, upstream_gradient.reshape(-1, channel_count))
        backward_signal = jnp.dot(dilated_convolution(upstream_gradient, DILATION_STEP, -1).reshape(-1, 9 * channel_count), rotated_kernel, preferred_element_type=jnp.float32).astype(jnp.bfloat16)
        masked = jnp.where(before > 0.0, backward_signal, jnp.zeros_like(backward_signal))
        grad_one = contract(near, masked)
        return (result.reshape(height, width, channel_count), grad_one, grad_two)
    outputs, grads_one, grads_two = lax.map(one_sample, (inputs, cotangent))
    factor = 1.0 / math.sqrt(samples * height * width)
    return (outputs, lax.optimization_barrier(jnp.sum(grads_one, axis=0)) * factor, lax.optimization_barrier(jnp.sum(grads_two, axis=0)) * factor)
```

```python
import functools
import math

import jax
import jax.numpy as jnp
from jax import lax
from jax.experimental import pallas as pl
from jax.experimental.pallas import tpu as pltpu
from jax.sharding import PartitionSpec as P

NEAR = 4
VMEM_LIMIT = 56 * 1024 * 1024
F32 = jnp.float32
BF16 = jnp.bfloat16


def edge_rows(block, width):
    count = lax.axis_size("rows")
    forward = [(i, i + 1) for i in range(count - 1)]
    backward = [(i + 1, i) for i in range(count - 1)]
    low = lax.ppermute(block[block.shape[0] - width :], "rows", forward)
    high = lax.ppermute(block[:width], "rows", backward)
    return low, high


def fill_padded(scratch, low, mid, high, margin):
    width, cols, channels = low.shape
    rows = mid.shape[0]
    side = jnp.zeros((scratch.shape[0], margin, channels), scratch.dtype)
    scratch[:, 0:margin, :] = side
    scratch[:, margin + cols : margin + cols + margin, :] = side
    scratch[0:width, margin : margin + cols, :] = low[...]
    scratch[width : width + rows, margin : margin + cols, :] = mid[...]
    scratch[width + rows : width + rows + width, margin : margin + cols, :] = high[...]


def fill_shifted(scratch, low, mid, high):
    width, cols, channels = low.shape
    rows = mid.shape[0]
    for ref, start, count in ((low, 0, width), (mid, width, rows), (high, width + rows, width)):

        @pl.loop(0, count)
        def _(r):
            line = ref[r].astype(F32)
            zero = jnp.zeros((NEAR, channels), F32)
            scratch[0, start + r] = jnp.concatenate([zero, line[: cols - NEAR]], axis=0).astype(BF16)
            scratch[1, start + r] = ref[r]
            scratch[2, start + r] = jnp.concatenate([line[NEAR:], zero], axis=0).astype(BF16)


def near_kernel(tile, low, mid, high, weight, hidden, shifted):
    step = pl.program_id(0)

    @pl.when(step == 0)
    def _():
        fill_shifted(shifted, low, mid, high)

    cols, channels = mid.shape[1:]
    pieces = []
    for a in range(3):
        for b in range(3):
            window = shifted[b, pl.ds(step * tile + a * NEAR, tile)]
            pieces.append(window.reshape(tile * cols, channels))
    before = jnp.dot(jnp.concatenate(pieces, axis=1), weight[...], preferred_element_type=F32)
    hidden[...] = jnp.maximum(before, 0.0).astype(BF16).reshape(tile, cols, channels)


def far_windows(padded, step, tile, spacing, cols, direction):
    pieces = []
    for a in (-1, 0, 1):
        for b in (-1, 0, 1):
            first_col = spacing + direction * b * spacing
            window = padded[
                pl.ds(step * tile + spacing + direction * a * spacing, tile),
                first_col : first_col + cols,
                :,
            ]
            pieces.append(window.reshape(tile * cols, padded.shape[-1]))
    return jnp.concatenate(pieces, axis=1)


def output_kernel(tile, spacing, low, mid, high, weight, out, padded):
    step = pl.program_id(0)

    @pl.when(step == 0)
    def _():
        fill_padded(padded, low, mid, high, spacing)

    cols, channels = mid.shape[1:]
    stacked = far_windows(padded, step, tile, spacing, cols, 1)
    result = jnp.dot(stacked, weight[...], preferred_element_type=F32)
    out[...] = result.astype(BF16).reshape(tile, cols, channels)


def back_kernel(tile, spacing, low, mid, high, weight, hidden, masked, padded, turned):
    step = pl.program_id(0)
    cols, channels = mid.shape[1:]

    @pl.when(step == 0)
    def _():
        fill_padded(padded, low, mid, high, spacing)
        for t in range(9):
            turned[t * channels : (t + 1) * channels, :] = weight[
                t * channels : (t + 1) * channels, :
            ].T

    stacked = far_windows(padded, step, tile, spacing, cols, -1)
    back = jnp.dot(stacked, turned[...], preferred_element_type=F32).astype(BF16)
    back = back.reshape(tile, cols, channels)
    masked[...] = jnp.where(hidden[...] > 0, back, jnp.zeros_like(back))


def far_grad_kernel(spacing, low, mid, high, hidden, out, padded, turned):
    tap = pl.program_id(0)
    rows, cols, channels = mid.shape

    @pl.when(tap == 0)
    def _():
        fill_padded(padded, low, mid, high, spacing)
        turned[...] = hidden[...].reshape(rows * cols, channels).T

    first_row = (2 - tap // 3) * spacing
    first_col = pl.multiple_of((2 - tap % 3) * spacing, 16)
    window = padded[pl.ds(first_row, rows), pl.ds(first_col, cols), :]
    out[...] = jnp.dot(
        turned[...], window.reshape(rows * cols, channels), preferred_element_type=F32
    )


def near_grad_kernel(low, mid, high, masked, out, shifted, turned):
    tap = pl.program_id(0)
    rows, cols, channels = mid.shape

    @pl.when(tap == 0)
    def _():
        fill_shifted(shifted, low, mid, high)
        turned[...] = masked[...].reshape(rows * cols, channels).T

    window = shifted[tap % 3, pl.ds((tap // 3) * NEAR, rows)]
    product = jnp.dot(
        turned[...], window.reshape(rows * cols, channels), preferred_element_type=F32
    )
    out[...] = product.T


def run(kernel, out_shape, grid, out_spec, scratch, args, specs, flops):
    whole = pl.BlockSpec(memory_space=pltpu.VMEM)
    return pl.pallas_call(
        kernel,
        out_shape=out_shape,
        grid=(grid,),
        in_specs=[whole if spec is None else spec for spec in specs],
        out_specs=out_spec,
        scratch_shapes=scratch,
        compiler_params=pltpu.CompilerParams(vmem_limit_bytes=VMEM_LIMIT),
        cost_estimate=pl.CostEstimate(
            flops=flops, bytes_accessed=12 * 1024 * 1024, transcendentals=0
        ),
    )(*args)


def halve(total, axis, bit):
    count = lax.axis_size(axis)
    mine = (lax.axis_index(axis) >> bit) & 1
    pairs = [(i, i ^ (1 << bit)) for i in range(count)]
    sent = lax.dynamic_index_in_dim(total, 1 - mine, 0, keepdims=False).astype(BF16)
    kept = lax.dynamic_index_in_dim(total, mine, 0, keepdims=False)
    return kept + lax.ppermute(sent, axis, pairs).astype(F32)


def reduce_grad(grad):
    rows, dp = lax.axis_size("rows"), lax.axis_size("dp")
    taps, channels = grad.shape
    height, width = taps // rows, channels // dp
    outer = rows // 2
    total = jnp.moveaxis(grad.reshape(outer, 2, height, channels), 1, 0)
    total = halve(total, "rows", 0).reshape(outer * height, channels).T
    for bit in reversed(range(dp.bit_length() - 1)):
        total = halve(total.reshape(2, total.shape[0] // 2, outer * height), "dp", bit)
    total = total.T.reshape(outer, height, width)
    for bit in reversed(range(1, rows.bit_length() - 1)):
        total = halve(total.reshape(2, total.shape[0] // 2, height, width), "rows", bit)
    return total.reshape(height, width)


def on_device(inputs, cotangent, weight_one, weight_two):
    picture, upstream = inputs[0], cotangent[0]
    rows, cols, channels = picture.shape
    group = lax.axis_size("rows")
    spacing = 2 * group
    factor = 1.0 / math.sqrt(lax.axis_size("dp") * rows * group * cols)
    flops = 2 * rows * cols * weight_one.shape[0] * channels
    tile = 8
    steps = rows // tile
    map_shape = jax.ShapeDtypeStruct((rows, cols, channels), BF16)
    map_spec = pl.BlockSpec((tile, cols, channels), lambda i: (i, 0, 0))
    grad_shape = jax.ShapeDtypeStruct(weight_one.shape, F32)
    grad_spec = pl.BlockSpec((channels, channels), lambda t: (t, 0))
    padded = pltpu.VMEM((rows + 2 * spacing, cols + 2 * spacing, channels), BF16)
    shifted = pltpu.VMEM((3, rows + 2 * NEAR, cols, channels), BF16)
    turned = pltpu.VMEM((channels, rows * cols), BF16)

    near_low, near_high = edge_rows(picture, NEAR)
    far_low, far_high = edge_rows(upstream, spacing)
    near = (near_low, picture, near_high)
    far = (far_low, upstream, far_high)

    hidden = run(
        functools.partial(near_kernel, tile),
        map_shape, steps, map_spec, [shifted],
        (*near, weight_one), [None] * 4, flops,
    )
    grad_two = run(
        functools.partial(far_grad_kernel, spacing),
        grad_shape, 9, grad_spec, [padded, turned],
        (*far, hidden), [None] * 4, flops,
    )
    masked = run(
        functools.partial(back_kernel, tile, spacing),
        map_shape, steps, map_spec, [padded, pltpu.VMEM(weight_two.shape, BF16)],
        (*far, weight_two, hidden), [None] * 4 + [map_spec], flops,
    )
    grad_one = run(
        near_grad_kernel,
        grad_shape, 9, grad_spec, [shifted, turned],
        (*near, masked), [None] * 4, flops,
    )
    hidden_low, hidden_high = edge_rows(hidden, spacing)
    output = run(
        functools.partial(output_kernel, tile, spacing),
        map_shape, steps, map_spec, [padded],
        (hidden_low, hidden, hidden_high, weight_two), [None] * 4, flops,
    )
    grad_two = reduce_grad(grad_two)
    grad_one = reduce_grad(grad_one)
    return (output[None], grad_one * factor, grad_two * factor)


def solution(mesh):
    return jax.shard_map(
        on_device,
        mesh=mesh,
        in_specs=(P("dp", "rows", None, None), P("dp", "rows", None, None), P(), P()),
        out_specs=(P("dp", "rows", None, None), P("rows", "dp"), P("rows", "dp")),
        check_vma=False,
    )
```

```python
import functools
import math

import jax
import jax.numpy as jnp
from jax import lax
from jax.experimental import pallas as pl
from jax.experimental.pallas import tpu as pltpu
from jax.sharding import PartitionSpec as P

NEAR = 4
VMEM_LIMIT = 56 * 1024 * 1024
F32 = jnp.float32
BF16 = jnp.bfloat16


def edge_rows(block, width):
    count = lax.axis_size("rows")
    forward = [(i, i + 1) for i in range(count - 1)]
    backward = [(i + 1, i) for i in range(count - 1)]
    low = lax.ppermute(block[block.shape[0] - width :], "rows", forward)
    high = lax.ppermute(block[:width], "rows", backward)
    return low, high


def fill_padded(scratch, low, mid, high, margin):
    width, cols, channels = low.shape
    rows = mid.shape[0]
    side = jnp.zeros((scratch.shape[0], margin, channels), scratch.dtype)
    scratch[:, 0:margin, :] = side
    scratch[:, margin + cols : margin + cols + margin, :] = side
    scratch[0:width, margin : margin + cols, :] = low[...]
    scratch[width : width + rows, margin : margin + cols, :] = mid[...]
    scratch[width + rows : width + rows + width, margin : margin + cols, :] = high[...]


def fill_shifted(scratch, low, mid, high):
    width, cols, channels = low.shape
    rows = mid.shape[0]
    for ref, start, count in ((low, 0, width), (mid, width, rows), (high, width + rows, width)):

        @pl.loop(0, count)
        def _(r):
            line = ref[r].astype(F32)
            zero = jnp.zeros((NEAR, channels), F32)
            scratch[0, start + r] = jnp.concatenate([zero, line[: cols - NEAR]], axis=0).astype(BF16)
            scratch[1, start + r] = ref[r]
            scratch[2, start + r] = jnp.concatenate([line[NEAR:], zero], axis=0).astype(BF16)


def near_kernel(tile, low, mid, high, weight, hidden, shifted):
    step = pl.program_id(0)

    @pl.when(step == 0)
    def _():
        fill_shifted(shifted, low, mid, high)

    cols, channels = mid.shape[1:]
    pieces = []
    for a in range(3):
        for b in range(3):
            window = shifted[b, pl.ds(step * tile + a * NEAR, tile)]
            pieces.append(window.reshape(tile * cols, channels))
    before = jnp.dot(jnp.concatenate(pieces, axis=1), weight[...], preferred_element_type=F32)
    hidden[...] = jnp.maximum(before, 0.0).astype(BF16).reshape(tile, cols, channels)


def far_windows(padded, step, tile, spacing, cols, direction):
    pieces = []
    for a in (-1, 0, 1):
        for b in (-1, 0, 1):
            first_col = spacing + direction * b * spacing
            window = padded[
                pl.ds(step * tile + spacing + direction * a * spacing, tile),
                first_col : first_col + cols,
                :,
            ]
            pieces.append(window.reshape(tile * cols, padded.shape[-1]))
    return jnp.concatenate(pieces, axis=1)


def output_kernel(tile, spacing, first, low, mid, high, weight, out, padded):
    step = pl.program_id(0)

    @pl.when(step == 0)
    def _():
        fill_padded(padded, low, mid, high, spacing)

    cols, channels = mid.shape[1:]
    stacked = far_windows(padded, first + step, tile, spacing, cols, 1)
    result = jnp.dot(stacked, weight[...], preferred_element_type=F32)
    out[...] = result.astype(BF16).reshape(tile, cols, channels)


def back_kernel(tile, spacing, low, mid, high, weight, hidden, masked, padded, turned):
    step = pl.program_id(0)
    cols, channels = mid.shape[1:]

    @pl.when(step == 0)
    def _():
        fill_padded(padded, low, mid, high, spacing)
        for t in range(9):
            turned[t * channels : (t + 1) * channels, :] = weight[
                t * channels : (t + 1) * channels, :
            ].T

    stacked = far_windows(padded, step, tile, spacing, cols, -1)
    back = jnp.dot(stacked, turned[...], preferred_element_type=F32).astype(BF16)
    back = back.reshape(tile, cols, channels)
    masked[...] = jnp.where(hidden[...] > 0, back, jnp.zeros_like(back))


def far_grad_kernel(spacing, low, mid, high, hidden, out, padded, turned):
    tap = pl.program_id(0)
    rows, cols, channels = mid.shape

    @pl.when(tap == 0)
    def _():
        fill_padded(padded, low, mid, high, spacing)
        turned[...] = hidden[...].reshape(rows * cols, channels).T

    first_row = (2 - tap // 3) * spacing
    first_col = pl.multiple_of((2 - tap % 3) * spacing, 16)
    window = padded[pl.ds(first_row, rows), pl.ds(first_col, cols), :]
    out[...] = jnp.dot(
        turned[...], window.reshape(rows * cols, channels), preferred_element_type=F32
    )


def near_grad_kernel(low, mid, high, masked, out, shifted, turned):
    tap = pl.program_id(0)
    rows, cols, channels = mid.shape

    @pl.when(tap == 0)
    def _():
        fill_shifted(shifted, low, mid, high)
        turned[...] = masked[...].reshape(rows * cols, channels).T

    window = shifted[tap % 3, pl.ds((tap // 3) * NEAR, rows)]
    product = jnp.dot(
        turned[...], window.reshape(rows * cols, channels), preferred_element_type=F32
    )
    out[...] = product.T


def run(kernel, out_shape, grid, out_spec, scratch, args, specs, flops, after=(), aliases=None):
    whole = pl.BlockSpec(memory_space=pltpu.VMEM)
    first, last = len(args), len(args) + len(after)

    def body(*refs):
        kernel(*refs[:first], *refs[last:])

    return pl.pallas_call(
        body,
        out_shape=out_shape,
        grid=(grid,),
        in_specs=[whole if spec is None else spec for spec in specs]
        + [pl.BlockSpec(memory_space=pl.ANY)] * len(after),
        out_specs=out_spec,
        scratch_shapes=scratch,
        input_output_aliases=aliases or {},
        compiler_params=pltpu.CompilerParams(vmem_limit_bytes=VMEM_LIMIT),
        cost_estimate=pl.CostEstimate(
            flops=flops // 64, bytes_accessed=1024, transcendentals=0
        ),
    )(*args, *after)


def shared(pieces, axis, shift):
    owners = pieces.shape[0]
    mine = lax.axis_index(axis) >> shift
    kept = lax.dynamic_index_in_dim(pieces, mine, 0, keepdims=False)
    sent = [
        lax.dynamic_index_in_dim(pieces, mine ^ k, 0, keepdims=False).astype(BF16)
        for k in range(1, owners)
    ]
    return kept, sent


def joined(kept, sent, axis, shift):
    count = lax.axis_size(axis)
    total = kept
    for k, piece in enumerate(sent, 1):
        pairs = [(i, i ^ (k << shift)) for i in range(count)]
        total = total + lax.ppermute(piece, axis, pairs).astype(F32)
    return total


def split_pair(grad):
    taps, channels = grad.shape
    rows = lax.axis_size("rows")
    pieces = jnp.moveaxis(grad.reshape(rows // 2, 2, taps // rows, channels), 1, 0)
    mine = lax.axis_index("rows") & 1
    kept = lax.dynamic_index_in_dim(pieces, mine, 0, keepdims=False)
    sent = lax.dynamic_index_in_dim(pieces, 1 - mine, 0, keepdims=False).astype(BF16)
    return kept, [sent]


def split_samples(kept, sent):
    total = joined(kept, sent, "rows", 0)
    dp = lax.axis_size("dp")
    channels = total.shape[-1]
    turned = total.reshape(-1, channels).T
    return shared(turned.reshape(dp, channels // dp, turned.shape[1]), "dp", 0)


def split_rows(kept, sent):
    total = joined(kept, sent, "dp", 0)
    outer = lax.axis_size("rows") // 2
    pieces = jnp.moveaxis(total.reshape(total.shape[0], outer, -1), 1, 0)
    return shared(pieces, "rows", 1)


def finish(kept, sent):
    return joined(kept, sent, "rows", 1).T


def on_device(inputs, cotangent, weight_one, weight_two):
    picture, upstream = inputs[0], cotangent[0]
    rows, cols, channels = picture.shape
    group = lax.axis_size("rows")
    spacing = 2 * group
    factor = 1.0 / math.sqrt(lax.axis_size("dp") * rows * group * cols)
    flops = 2 * rows * cols * weight_one.shape[0] * channels
    tile = 8
    steps = rows // tile
    map_shape = jax.ShapeDtypeStruct((rows, cols, channels), BF16)
    map_spec = pl.BlockSpec((tile, cols, channels), lambda i: (i, 0, 0))
    grad_shape = jax.ShapeDtypeStruct(weight_one.shape, F32)
    grad_spec = pl.BlockSpec((channels, channels), lambda t: (t, 0))
    padded = pltpu.VMEM((rows + 2 * spacing, cols + 2 * spacing, channels), BF16)
    shifted = pltpu.VMEM((3, rows + 2 * NEAR, cols, channels), BF16)
    turned = pltpu.VMEM((channels, rows * cols), BF16)

    near_low, near_high = edge_rows(picture, NEAR)
    far_low, far_high = edge_rows(upstream, spacing)
    near = (near_low, picture, near_high)
    far = (far_low, upstream, far_high)

    hidden = run(
        functools.partial(near_kernel, tile),
        map_shape, steps, map_spec, [shifted],
        (*near, weight_one), [None] * 4, flops,
    )
    hidden_low, hidden_high = edge_rows(hidden, spacing)
    grad_two = run(
        functools.partial(far_grad_kernel, spacing),
        grad_shape, 9, grad_spec, [padded, turned],
        (*far, hidden), [None] * 4, flops,
    )
    pair_two = split_pair(grad_two)
    masked = run(
        functools.partial(back_kernel, tile, spacing),
        map_shape, steps, map_spec, [padded, pltpu.VMEM(weight_two.shape, BF16)],
        (*far, weight_two, hidden), [None] * 4 + [map_spec], flops, pair_two[1],
    )
    samples_two = split_samples(*pair_two)
    grad_one = run(
        near_grad_kernel,
        grad_shape, 9, grad_spec, [shifted, turned],
        (*near, masked), [None] * 4, flops, samples_two[1],
    )
    pair_one = split_pair(grad_one)
    rows_two = split_rows(*samples_two)
    early = max(1, steps // 4)
    output = run(
        functools.partial(output_kernel, tile, spacing, 0),
        map_shape, early, map_spec, [padded],
        (hidden_low, hidden, hidden_high, weight_two), [None] * 4,
        flops * early // steps, pair_one[1] + rows_two[1],
    )
    kept_one, output = lax.optimization_barrier((pair_one[0], output))
    samples_one = split_samples(kept_one, pair_one[1])
    if early < steps:
        output = run(
            functools.partial(output_kernel, tile, spacing, early),
            map_shape, steps - early,
            pl.BlockSpec((tile, cols, channels), lambda i: (i + early, 0, 0)), [padded],
            (hidden_low, hidden, hidden_high, weight_two), [None] * 4,
            flops * (steps - early) // steps, [output] + samples_one[1], {4: 0},
        )
    grad_two = finish(*rows_two)
    grad_one = finish(*split_rows(*samples_one))
    return (output[None], grad_one * factor, grad_two * factor)


def solution(mesh):
    return jax.shard_map(
        on_device,
        mesh=mesh,
        in_specs=(P("dp", "rows", None, None), P("dp", "rows", None, None), P(), P()),
        out_specs=(P("dp", "rows", None, None), P("rows", "dp"), P("rows", "dp")),
        check_vma=False,
    )
```

```python
import functools
import math

import jax
import jax.numpy as jnp
from jax import lax
from jax.experimental import pallas as pl
from jax.experimental.pallas import tpu as pltpu
from jax.sharding import PartitionSpec as P

NEAR = 4
VMEM_LIMIT = 56 * 1024 * 1024
F32 = jnp.float32
BF16 = jnp.bfloat16


def edge_rows(block, width):
    count = lax.axis_size("rows")
    forward = [(i, i + 1) for i in range(count - 1)]
    backward = [(i + 1, i) for i in range(count - 1)]
    low = lax.ppermute(block[block.shape[0] - width :], "rows", forward)
    high = lax.ppermute(block[:width], "rows", backward)
    return low, high


def fill_padded(scratch, low, mid, high, margin):
    width, cols, channels = low.shape
    rows = mid.shape[0]
    side = jnp.zeros((scratch.shape[0], margin, channels), scratch.dtype)
    scratch[:, 0:margin, :] = side
    scratch[:, margin + cols : margin + cols + margin, :] = side
    scratch[0:width, margin : margin + cols, :] = low[...]
    scratch[width : width + rows, margin : margin + cols, :] = mid[...]
    scratch[width + rows : width + rows + width, margin : margin + cols, :] = high[...]


def fill_shifted(scratch, low, mid, high):
    width, cols, channels = low.shape
    rows = mid.shape[0]
    for ref, start, count in ((low, 0, width), (mid, width, rows), (high, width + rows, width)):

        @pl.loop(0, count)
        def _(r):
            line = ref[r].astype(F32)
            zero = jnp.zeros((NEAR, channels), F32)
            scratch[0, start + r] = jnp.concatenate([zero, line[: cols - NEAR]], axis=0).astype(BF16)
            scratch[1, start + r] = ref[r]
            scratch[2, start + r] = jnp.concatenate([line[NEAR:], zero], axis=0).astype(BF16)


def flat_product(matrix, stacked):
    product = lax.dot_general(
        matrix, stacked, (((1,), (1,)), ((), ())), preferred_element_type=F32
    )
    return product.T


def near_kernel(tile, low, mid, high, weight, hidden, shifted, matrix):
    step = pl.program_id(0)

    @pl.when(step == 0)
    def _():
        matrix[...] = weight[...].T
        fill_shifted(shifted, low, mid, high)

    cols, channels = mid.shape[1:]
    pieces = []
    for a in range(3):
        for b in range(3):
            window = shifted[b, pl.ds(step * tile + a * NEAR, tile)]
            pieces.append(window.reshape(tile * cols, channels))
    before = flat_product(matrix[...], jnp.concatenate(pieces, axis=1))
    hidden[...] = jnp.maximum(before, 0.0).astype(BF16).reshape(tile, cols, channels)


def far_windows(padded, step, tile, spacing, cols, direction):
    pieces = []
    for a in (-1, 0, 1):
        for b in (-1, 0, 1):
            first_col = spacing + direction * b * spacing
            window = padded[
                pl.ds(step * tile + spacing + direction * a * spacing, tile),
                first_col : first_col + cols,
                :,
            ]
            pieces.append(window.reshape(tile * cols, padded.shape[-1]))
    return jnp.concatenate(pieces, axis=1)


def output_kernel(tile, spacing, first, low, mid, high, weight, out, padded, matrix):
    step = pl.program_id(0)

    @pl.when(step == 0)
    def _():
        matrix[...] = weight[...].T
        fill_padded(padded, low, mid, high, spacing)

    cols, channels = mid.shape[1:]
    stacked = far_windows(padded, first + step, tile, spacing, cols, 1)
    result = flat_product(matrix[...], stacked)
    out[...] = result.astype(BF16).reshape(tile, cols, channels)


def back_kernel(tile, spacing, low, mid, high, weight, hidden, masked, padded, turned):
    step = pl.program_id(0)
    cols, channels = mid.shape[1:]

    @pl.when(step == 0)
    def _():
        fill_padded(padded, low, mid, high, spacing)
        for t in range(9):
            turned[:, t * channels : (t + 1) * channels] = weight[
                t * channels : (t + 1) * channels, :
            ]

    stacked = far_windows(padded, step, tile, spacing, cols, -1)
    back = flat_product(turned[...], stacked).astype(BF16)
    back = back.reshape(tile, cols, channels)
    masked[...] = jnp.where(hidden[...] > 0, back, jnp.zeros_like(back))


def far_grad_kernel(spacing, low, mid, high, hidden, out, padded, turned):
    a = pl.program_id(0)
    rows, cols, channels = mid.shape

    @pl.when(a == 0)
    def _():
        fill_padded(padded, low, mid, high, spacing)
        turned[...] = hidden[...].reshape(rows * cols, channels).T

    windows = [
        padded[
            pl.ds((2 - a) * spacing, rows), (2 - b) * spacing : (2 - b) * spacing + cols, :
        ].reshape(rows * cols, channels)
        for b in range(3)
    ]
    product = jnp.dot(
        turned[...], jnp.concatenate(windows, axis=1), preferred_element_type=F32
    )
    for b in range(3):
        out[b * channels : (b + 1) * channels, :] = product[:, b * channels : (b + 1) * channels]


def near_grad_kernel(low, mid, high, masked, out, shifted, turned):
    a = pl.program_id(0)
    rows, cols, channels = mid.shape

    @pl.when(a == 0)
    def _():
        fill_shifted(shifted, low, mid, high)
        turned[...] = masked[...].reshape(rows * cols, channels).T

    windows = [
        shifted[b, pl.ds(a * NEAR, rows)].reshape(rows * cols, channels) for b in range(3)
    ]
    product = jnp.dot(
        turned[...], jnp.concatenate(windows, axis=1), preferred_element_type=F32
    )
    out[...] = product.T


def run(kernel, out_shape, grid, out_spec, scratch, args, specs, flops, after=(), aliases=None):
    whole = pl.BlockSpec(memory_space=pltpu.VMEM)
    first, last = len(args), len(args) + len(after)

    def body(*refs):
        kernel(*refs[:first], *refs[last:])

    return pl.pallas_call(
        body,
        out_shape=out_shape,
        grid=(grid,),
        in_specs=[whole if spec is None else spec for spec in specs]
        + [pl.BlockSpec(memory_space=pl.ANY)] * len(after),
        out_specs=out_spec,
        scratch_shapes=scratch,
        input_output_aliases=aliases or {},
        compiler_params=pltpu.CompilerParams(vmem_limit_bytes=VMEM_LIMIT),
        cost_estimate=pl.CostEstimate(
            flops=flops // 64, bytes_accessed=1024, transcendentals=0
        ),
    )(*args, *after)


def shared(pieces, axis, shift):
    owners = pieces.shape[0]
    mine = lax.axis_index(axis) >> shift
    kept = lax.dynamic_index_in_dim(pieces, mine, 0, keepdims=False)
    sent = [
        lax.dynamic_index_in_dim(pieces, mine ^ k, 0, keepdims=False).astype(BF16)
        for k in range(1, owners)
    ]
    return kept, sent


def joined(kept, sent, axis, shift):
    count = lax.axis_size(axis)
    total = kept
    for k, piece in enumerate(sent, 1):
        pairs = [(i, i ^ (k << shift)) for i in range(count)]
        total = total + lax.ppermute(piece, axis, pairs).astype(F32)
    return total


def split_pair(grad):
    taps, channels = grad.shape
    rows = lax.axis_size("rows")
    pieces = jnp.moveaxis(grad.reshape(rows // 2, 2, taps // rows, channels), 1, 0)
    mine = lax.axis_index("rows") & 1
    kept = lax.dynamic_index_in_dim(pieces, mine, 0, keepdims=False)
    sent = lax.dynamic_index_in_dim(pieces, 1 - mine, 0, keepdims=False).astype(BF16)
    return kept, [sent]


def split_samples(kept, sent):
    total = joined(kept, sent, "rows", 0)
    dp = lax.axis_size("dp")
    channels = total.shape[-1]
    turned = total.reshape(-1, channels).T
    return shared(turned.reshape(dp, channels // dp, turned.shape[1]), "dp", 0)


def reduce_rows(*totals):
    outer = lax.axis_size("rows") // 2
    pieces = [jnp.moveaxis(t.reshape(t.shape[0], outer, -1), 1, 0) for t in totals]
    height = pieces[0].shape[1]
    total = joined(*shared(jnp.concatenate(pieces, axis=1), "rows", 1), "rows", 1)
    return [total[i * height : (i + 1) * height].T for i in range(len(totals))]


def on_device(inputs, cotangent, weight_one, weight_two):
    picture, upstream = inputs[0], cotangent[0]
    rows, cols, channels = picture.shape
    group = lax.axis_size("rows")
    spacing = 2 * group
    factor = 1.0 / math.sqrt(lax.axis_size("dp") * rows * group * cols)
    flops = 2 * rows * cols * weight_one.shape[0] * channels
    tile = 8
    steps = rows // tile
    map_shape = jax.ShapeDtypeStruct((rows, cols, channels), BF16)
    map_spec = pl.BlockSpec((tile, cols, channels), lambda i: (i, 0, 0))
    grad_shape = jax.ShapeDtypeStruct(weight_one.shape, F32)
    grad_spec = pl.BlockSpec((3 * channels, channels), lambda a: (a, 0))
    padded = pltpu.VMEM((rows + 2 * spacing, cols + 2 * spacing, channels), BF16)
    shifted = pltpu.VMEM((3, rows + 2 * NEAR, cols, channels), BF16)
    turned = pltpu.VMEM((channels, rows * cols), BF16)
    matrix = pltpu.VMEM(weight_one.shape[::-1], BF16)

    near_low, near_high = edge_rows(picture, NEAR)
    far_low, far_high = edge_rows(upstream, spacing)
    near = (near_low, picture, near_high)
    far = (far_low, upstream, far_high)

    hidden = run(
        functools.partial(near_kernel, tile),
        map_shape, steps, map_spec, [shifted, matrix],
        (*near, weight_one), [None] * 4, flops,
    )
    hidden_low, hidden_high = edge_rows(hidden, spacing)
    grad_two = run(
        functools.partial(far_grad_kernel, spacing),
        grad_shape, 3, grad_spec, [padded, turned],
        (*far, hidden), [None] * 4, flops,
    )
    pair_two = split_pair(grad_two)
    masked = run(
        functools.partial(back_kernel, tile, spacing),
        map_shape, steps, map_spec, [padded, matrix],
        (*far, weight_two, hidden), [None] * 4 + [map_spec], flops, pair_two[1],
    )
    samples_two = split_samples(*pair_two)
    grad_one = run(
        near_grad_kernel,
        grad_shape, 3, grad_spec, [shifted, turned],
        (*near, masked), [None] * 4, flops, samples_two[1],
    )
    pair_one = split_pair(grad_one)
    early = max(1, steps // 4)
    output = run(
        functools.partial(output_kernel, tile, spacing, 0),
        map_shape, early, map_spec, [padded, matrix],
        (hidden_low, hidden, hidden_high, weight_two), [None] * 4,
        flops * early // steps, pair_one[1],
    )
    kept_one, kept_two, output = lax.optimization_barrier((pair_one[0], samples_two[0], output))
    samples_one = split_samples(kept_one, pair_one[1])
    total_two = joined(kept_two, samples_two[1], "dp", 0)
    if early < steps:
        output = run(
            functools.partial(output_kernel, tile, spacing, early),
            map_shape, steps - early,
            pl.BlockSpec((tile, cols, channels), lambda i: (i + early, 0, 0)), [padded, matrix],
            (hidden_low, hidden, hidden_high, weight_two), [None] * 4,
            flops * (steps - early) // steps, [output] + samples_one[1], {4: 0},
        )
    kept_one, total_two, output = lax.optimization_barrier((samples_one[0], total_two, output))
    total_one = joined(kept_one, samples_one[1], "dp", 0)
    grad_one, grad_two = reduce_rows(total_one, total_two)
    return (output[None], grad_one * factor, grad_two * factor)


def solution(mesh):
    return jax.shard_map(
        on_device,
        mesh=mesh,
        in_specs=(P("dp", "rows", None, None), P("dp", "rows", None, None), P(), P()),
        out_specs=(P("dp", "rows", None, None), P("rows", "dp"), P("rows", "dp")),
        check_vma=False,
    )
```

```python
import functools
import math

import jax
import jax.numpy as jnp
from jax import lax
from jax.experimental import pallas as pl
from jax.experimental.pallas import tpu as pltpu
from jax.sharding import PartitionSpec as P

NEAR = 4
VMEM_LIMIT = 56 * 1024 * 1024
F32 = jnp.float32
BF16 = jnp.bfloat16


def edge_rows(block, width):
    count = lax.axis_size("rows")
    forward = [(i, i + 1) for i in range(count - 1)]
    backward = [(i + 1, i) for i in range(count - 1)]
    low = lax.ppermute(block[block.shape[0] - width :], "rows", forward)
    high = lax.ppermute(block[:width], "rows", backward)
    return low, high


def fill_padded(scratch, low, mid, high, margin):
    width, cols, channels = low.shape
    rows = mid.shape[0]
    side = jnp.zeros((scratch.shape[0], margin, channels), scratch.dtype)
    scratch[:, 0:margin, :] = side
    scratch[:, margin + cols : margin + cols + margin, :] = side
    scratch[0:width, margin : margin + cols, :] = low[...]
    scratch[width : width + rows, margin : margin + cols, :] = mid[...]
    scratch[width + rows : width + rows + width, margin : margin + cols, :] = high[...]


def fill_shifted(scratch, low, mid, high):
    width, cols, channels = low.shape
    rows = mid.shape[0]
    for ref, start, count in ((low, 0, width), (mid, width, rows), (high, width + rows, width)):

        @pl.loop(0, count)
        def _(r):
            line = ref[r].astype(F32)
            zero = jnp.zeros((NEAR, channels), F32)
            scratch[0, start + r] = jnp.concatenate([zero, line[: cols - NEAR]], axis=0).astype(BF16)
            scratch[1, start + r] = ref[r]
            scratch[2, start + r] = jnp.concatenate([line[NEAR:], zero], axis=0).astype(BF16)


def flat_product(matrix, stacked):
    product = lax.dot_general(
        matrix, stacked, (((1,), (1,)), ((), ())), preferred_element_type=F32
    )
    return product.T


def near_kernel(tile, low, mid, high, weight, hidden, shifted, matrix):
    step = pl.program_id(0)

    @pl.when(step == 0)
    def _():
        matrix[...] = weight[...].T
        fill_shifted(shifted, low, mid, high)

    cols, channels = mid.shape[1:]
    pieces = []
    for a in range(3):
        for b in range(3):
            window = shifted[b, pl.ds(step * tile + a * NEAR, tile)]
            pieces.append(window.reshape(tile * cols, channels))
    before = flat_product(matrix[...], jnp.concatenate(pieces, axis=1))
    hidden[...] = jnp.maximum(before, 0.0).astype(BF16).reshape(tile, cols, channels)


def far_windows(padded, step, tile, spacing, cols, direction):
    pieces = []
    for a in (-1, 0, 1):
        for b in (-1, 0, 1):
            first_col = spacing + direction * b * spacing
            window = padded[
                pl.ds(step * tile + spacing + direction * a * spacing, tile),
                first_col : first_col + cols,
                :,
            ]
            pieces.append(window.reshape(tile * cols, padded.shape[-1]))
    return jnp.concatenate(pieces, axis=1)


def output_kernel(tile, spacing, first, low, mid, high, weight, out, padded, matrix):
    step = pl.program_id(0)

    @pl.when(step == 0)
    def _():
        matrix[...] = weight[...].T
        fill_padded(padded, low, mid, high, spacing)

    cols, channels = mid.shape[1:]
    stacked = far_windows(padded, first + step, tile, spacing, cols, 1)
    result = flat_product(matrix[...], stacked)
    out[...] = result.astype(BF16).reshape(tile, cols, channels)


def back_kernel(tile, spacing, low, mid, high, weight, hidden, masked, padded, turned):
    step = pl.program_id(0)
    cols, channels = mid.shape[1:]

    @pl.when(step == 0)
    def _():
        fill_padded(padded, low, mid, high, spacing)
        for t in range(9):
            turned[:, t * channels : (t + 1) * channels] = weight[
                t * channels : (t + 1) * channels, :
            ]

    stacked = far_windows(padded, step, tile, spacing, cols, -1)
    back = flat_product(turned[...], stacked).astype(BF16)
    back = back.reshape(tile, cols, channels)
    masked[...] = jnp.where(hidden[...] > 0, back, jnp.zeros_like(back))


def far_grad_kernel(spacing, low, mid, high, hidden, out, padded, turned):
    a = pl.program_id(0)
    rows, cols, channels = mid.shape

    @pl.when(a == 0)
    def _():
        fill_padded(padded, low, mid, high, spacing)
        turned[...] = hidden[...].reshape(rows * cols, channels).T

    windows = [
        padded[
            pl.ds((2 - a) * spacing, rows), (2 - b) * spacing : (2 - b) * spacing + cols, :
        ].reshape(rows * cols, channels)
        for b in range(3)
    ]
    product = jnp.dot(
        turned[...], jnp.concatenate(windows, axis=1), preferred_element_type=F32
    )
    for b in range(3):
        out[b * channels : (b + 1) * channels, :] = product[:, b * channels : (b + 1) * channels]


def near_grad_kernel(low, mid, high, masked, out, shifted, turned):
    a = pl.program_id(0)
    rows, cols, channels = mid.shape

    @pl.when(a == 0)
    def _():
        fill_shifted(shifted, low, mid, high)
        turned[...] = masked[...].reshape(rows * cols, channels).T

    windows = [
        shifted[b, pl.ds(a * NEAR, rows)].reshape(rows * cols, channels) for b in range(3)
    ]
    product = jnp.dot(
        turned[...], jnp.concatenate(windows, axis=1), preferred_element_type=F32
    )
    out[...] = product.T


def run(kernel, out_shape, grid, out_spec, scratch, args, specs, flops, after=(), aliases=None):
    whole = pl.BlockSpec(memory_space=pltpu.VMEM)
    first, last = len(args), len(args) + len(after)

    def body(*refs):
        kernel(*refs[:first], *refs[last:])

    return pl.pallas_call(
        body,
        out_shape=out_shape,
        grid=(grid,),
        in_specs=[whole if spec is None else spec for spec in specs]
        + [pl.BlockSpec(memory_space=pl.ANY)] * len(after),
        out_specs=out_spec,
        scratch_shapes=scratch,
        input_output_aliases=aliases or {},
        compiler_params=pltpu.CompilerParams(vmem_limit_bytes=VMEM_LIMIT),
        cost_estimate=pl.CostEstimate(
            flops=flops // 64, bytes_accessed=1024, transcendentals=0
        ),
    )(*args, *after)


def shared(pieces, axis, shift):
    owners = pieces.shape[0]
    mine = lax.axis_index(axis) >> shift
    kept = lax.dynamic_index_in_dim(pieces, mine, 0, keepdims=False)
    sent = [
        lax.dynamic_index_in_dim(pieces, mine ^ k, 0, keepdims=False).astype(BF16)
        for k in range(1, owners)
    ]
    return kept, sent


def joined(kept, sent, axis, shift):
    count = lax.axis_size(axis)
    total = kept
    for k, piece in enumerate(sent, 1):
        pairs = [(i, i ^ (k << shift)) for i in range(count)]
        total = total + lax.ppermute(piece, axis, pairs).astype(F32)
    return total


def split_pair(grad):
    taps, channels = grad.shape
    rows = lax.axis_size("rows")
    pieces = jnp.moveaxis(grad.reshape(rows // 2, 2, taps // rows, channels), 1, 0)
    mine = lax.axis_index("rows") & 1
    kept = lax.dynamic_index_in_dim(pieces, mine, 0, keepdims=False)
    sent = lax.dynamic_index_in_dim(pieces, 1 - mine, 0, keepdims=False).astype(BF16)
    return kept, [sent]


def split_samples(kept, sent):
    total = joined(kept, sent, "rows", 0)
    dp = lax.axis_size("dp")
    channels = total.shape[-1]
    turned = total.reshape(-1, channels).T
    return shared(turned.reshape(dp, channels // dp, turned.shape[1]), "dp", 0)


def split_rows(total):
    outer = lax.axis_size("rows") // 2
    pieces = jnp.moveaxis(total.reshape(total.shape[0], outer, -1), 1, 0)
    return shared(pieces, "rows", 1)


def on_device(inputs, cotangent, weight_one, weight_two):
    picture, upstream = inputs[0], cotangent[0]
    rows, cols, channels = picture.shape
    group = lax.axis_size("rows")
    spacing = 2 * group
    factor = 1.0 / math.sqrt(lax.axis_size("dp") * rows * group * cols)
    flops = 2 * rows * cols * weight_one.shape[0] * channels
    tile = 8
    steps = rows // tile
    map_shape = jax.ShapeDtypeStruct((rows, cols, channels), BF16)
    map_spec = pl.BlockSpec((tile, cols, channels), lambda i: (i, 0, 0))
    grad_shape = jax.ShapeDtypeStruct(weight_one.shape, F32)
    grad_spec = pl.BlockSpec((3 * channels, channels), lambda a: (a, 0))
    padded = pltpu.VMEM((rows + 2 * spacing, cols + 2 * spacing, channels), BF16)
    shifted = pltpu.VMEM((3, rows + 2 * NEAR, cols, channels), BF16)
    turned = pltpu.VMEM((channels, rows * cols), BF16)
    matrix = pltpu.VMEM(weight_one.shape[::-1], BF16)

    near_low, near_high = edge_rows(picture, NEAR)
    far_low, far_high = edge_rows(upstream, spacing)
    near = (near_low, picture, near_high)
    far = (far_low, upstream, far_high)

    hidden = run(
        functools.partial(near_kernel, tile),
        map_shape, steps, map_spec, [shifted, matrix],
        (*near, weight_one), [None] * 4, flops,
    )
    hidden_low, hidden_high = edge_rows(hidden, spacing)
    grad_two = run(
        functools.partial(far_grad_kernel, spacing),
        grad_shape, 3, grad_spec, [padded, turned],
        (*far, hidden), [None] * 4, flops,
    )
    pair_two = split_pair(grad_two)
    masked = run(
        functools.partial(back_kernel, tile, spacing),
        map_shape, steps, map_spec, [padded, matrix],
        (*far, weight_two, hidden), [None] * 4 + [map_spec], flops, pair_two[1],
    )
    samples_two = split_samples(*pair_two)
    grad_one = run(
        near_grad_kernel,
        grad_shape, 3, grad_spec, [shifted, turned],
        (*near, masked), [None] * 4, flops, samples_two[1],
    )
    pair_one = split_pair(grad_one)
    early = max(1, steps // 4)
    output = run(
        functools.partial(output_kernel, tile, spacing, 0),
        map_shape, early, map_spec, [padded, matrix],
        (hidden_low, hidden, hidden_high, weight_two), [None] * 4,
        flops * early // steps, pair_one[1],
    )
    kept_one, kept_two, output = lax.optimization_barrier((pair_one[0], samples_two[0], output))
    samples_one = split_samples(kept_one, pair_one[1])
    rows_two = split_rows(joined(kept_two, samples_two[1], "dp", 0))
    if early < steps:
        output = run(
            functools.partial(output_kernel, tile, spacing, early),
            map_shape, steps - early,
            pl.BlockSpec((tile, cols, channels), lambda i: (i + early, 0, 0)), [padded, matrix],
            (hidden_low, hidden, hidden_high, weight_two), [None] * 4,
            flops * (steps - early) // steps, [output] + samples_one[1] + rows_two[1], {4: 0},
        )
    kept_one, kept_two, output = lax.optimization_barrier((samples_one[0], rows_two[0], output))
    rows_one = split_rows(joined(kept_one, samples_one[1], "dp", 0))
    grad_two = joined(kept_two, rows_two[1], "rows", 1).T
    grad_one = joined(*rows_one, "rows", 1).T
    return (output[None], grad_one * factor, grad_two * factor)


def solution(mesh):
    return jax.shard_map(
        on_device,
        mesh=mesh,
        in_specs=(P("dp", "rows", None, None), P("dp", "rows", None, None), P(), P()),
        out_specs=(P("dp", "rows", None, None), P("rows", "dp"), P("rows", "dp")),
        check_vma=False,
    )
```

```python
import functools
import math

import jax
import jax.numpy as jnp
from jax import lax
from jax.experimental import pallas as pl
from jax.experimental.pallas import tpu as pltpu
from jax.sharding import PartitionSpec as P

NEAR = 4
VMEM_LIMIT = 56 * 1024 * 1024
F32 = jnp.float32
BF16 = jnp.bfloat16


def edge_rows(block, width):
    count = lax.axis_size("rows")
    forward = [(i, i + 1) for i in range(count - 1)]
    backward = [(i + 1, i) for i in range(count - 1)]
    low = lax.ppermute(block[block.shape[0] - width :], "rows", forward)
    high = lax.ppermute(block[:width], "rows", backward)
    return low, high


def fill_padded(scratch, low, mid, high, margin):
    width, cols, channels = low.shape
    rows = mid.shape[0]
    side = jnp.zeros((scratch.shape[0], margin, channels), scratch.dtype)
    scratch[:, 0:margin, :] = side
    scratch[:, margin + cols : margin + cols + margin, :] = side
    scratch[0:width, margin : margin + cols, :] = low[...]
    scratch[width : width + rows, margin : margin + cols, :] = mid[...]
    scratch[width + rows : width + rows + width, margin : margin + cols, :] = high[...]


def fill_shifted(scratch, low, mid, high):
    width, cols, channels = low.shape
    rows = mid.shape[0]
    for ref, start, count in ((low, 0, width), (mid, width, rows), (high, width + rows, width)):

        @pl.loop(0, count)
        def _(r):
            line = ref[r].astype(F32)
            zero = jnp.zeros((NEAR, channels), F32)
            scratch[0, start + r] = jnp.concatenate([zero, line[: cols - NEAR]], axis=0).astype(BF16)
            scratch[1, start + r] = ref[r]
            scratch[2, start + r] = jnp.concatenate([line[NEAR:], zero], axis=0).astype(BF16)


def flat_product(matrix, stacked):
    product = lax.dot_general(
        matrix, stacked, (((1,), (1,)), ((), ())), preferred_element_type=F32
    )
    return product.T


def near_kernel(tile, low, mid, high, weight, hidden, shifted, matrix):
    step = pl.program_id(0)

    @pl.when(step == 0)
    def _():
        matrix[...] = weight[...].T
        fill_shifted(shifted, low, mid, high)

    cols, channels = mid.shape[1:]
    pieces = []
    for a in range(3):
        for b in range(3):
            window = shifted[b, pl.ds(step * tile + a * NEAR, tile)]
            pieces.append(window.reshape(tile * cols, channels))
    before = flat_product(matrix[...], jnp.concatenate(pieces, axis=1))
    hidden[...] = jnp.maximum(before, 0.0).astype(BF16).reshape(tile, cols, channels)


def far_windows(padded, step, tile, spacing, cols, direction):
    pieces = []
    for a in (-1, 0, 1):
        for b in (-1, 0, 1):
            first_col = spacing + direction * b * spacing
            window = padded[
                pl.ds(step * tile + spacing + direction * a * spacing, tile),
                first_col : first_col + cols,
                :,
            ]
            pieces.append(window.reshape(tile * cols, padded.shape[-1]))
    return jnp.concatenate(pieces, axis=1)


def output_kernel(tile, spacing, first, low, mid, high, weight, out, padded, matrix):
    step = pl.program_id(0)

    @pl.when(step == 0)
    def _():
        matrix[...] = weight[...].T
        fill_padded(padded, low, mid, high, spacing)

    cols, channels = mid.shape[1:]
    stacked = far_windows(padded, first + step, tile, spacing, cols, 1)
    result = flat_product(matrix[...], stacked)
    out[...] = result.astype(BF16).reshape(tile, cols, channels)


def back_kernel(tile, spacing, low, mid, high, weight, hidden, masked, padded, turned):
    step = pl.program_id(0)
    cols, channels = mid.shape[1:]

    @pl.when(step == 0)
    def _():
        fill_padded(padded, low, mid, high, spacing)
        for t in range(9):
            turned[:, t * channels : (t + 1) * channels] = weight[
                t * channels : (t + 1) * channels, :
            ]

    stacked = far_windows(padded, step, tile, spacing, cols, -1)
    back = flat_product(turned[...], stacked).astype(BF16)
    back = back.reshape(tile, cols, channels)
    masked[...] = jnp.where(hidden[...] > 0, back, jnp.zeros_like(back))


def far_grad_kernel(spacing, low, mid, high, hidden, out, padded, turned):
    a = pl.program_id(0)
    rows, cols, channels = mid.shape

    @pl.when(a == 0)
    def _():
        fill_padded(padded, low, mid, high, spacing)
        turned[...] = hidden[...].reshape(rows * cols, channels).T

    windows = [
        padded[
            pl.ds((2 - a) * spacing, rows), (2 - b) * spacing : (2 - b) * spacing + cols, :
        ].reshape(rows * cols, channels)
        for b in range(3)
    ]
    product = jnp.dot(
        turned[...], jnp.concatenate(windows, axis=1), preferred_element_type=F32
    )
    for b in range(3):
        out[b * channels : (b + 1) * channels, :] = product[:, b * channels : (b + 1) * channels]


def near_grad_kernel(low, mid, high, masked, out, shifted, turned):
    a = pl.program_id(0)
    rows, cols, channels = mid.shape

    @pl.when(a == 0)
    def _():
        fill_shifted(shifted, low, mid, high)
        turned[...] = masked[...].reshape(rows * cols, channels).T

    windows = [
        shifted[b, pl.ds(a * NEAR, rows)].reshape(rows * cols, channels) for b in range(3)
    ]
    product = jnp.dot(
        turned[...], jnp.concatenate(windows, axis=1), preferred_element_type=F32
    )
    out[...] = product.T


def run(kernel, out_shape, grid, out_spec, scratch, args, specs, flops, after=(), aliases=None):
    whole = pl.BlockSpec(memory_space=pltpu.VMEM)
    first, last = len(args), len(args) + len(after)

    def body(*refs):
        kernel(*refs[:first], *refs[last:])

    return pl.pallas_call(
        body,
        out_shape=out_shape,
        grid=(grid,),
        in_specs=[whole if spec is None else spec for spec in specs]
        + [pl.BlockSpec(memory_space=pl.ANY)] * len(after),
        out_specs=out_spec,
        scratch_shapes=scratch,
        input_output_aliases=aliases or {},
        compiler_params=pltpu.CompilerParams(vmem_limit_bytes=VMEM_LIMIT),
        cost_estimate=pl.CostEstimate(
            flops=flops // 64, bytes_accessed=1024, transcendentals=0
        ),
    )(*args, *after)


def shared(pieces, axis, shift):
    owners = pieces.shape[0]
    mine = lax.axis_index(axis) >> shift
    kept = lax.dynamic_index_in_dim(pieces, mine, 0, keepdims=False)
    sent = [
        lax.dynamic_index_in_dim(pieces, mine ^ k, 0, keepdims=False).astype(BF16)
        for k in range(1, owners)
    ]
    return kept, sent


def joined(kept, sent, axis, shift):
    count = lax.axis_size(axis)
    total = kept
    for k, piece in enumerate(sent, 1):
        pairs = [(i, i ^ (k << shift)) for i in range(count)]
        total = total + lax.ppermute(piece, axis, pairs).astype(F32)
    return total


def split_pair(grad):
    taps, channels = grad.shape
    rows = lax.axis_size("rows")
    pieces = jnp.moveaxis(grad.reshape(rows // 2, 2, taps // rows, channels), 1, 0)
    mine = lax.axis_index("rows") & 1
    kept = lax.dynamic_index_in_dim(pieces, mine, 0, keepdims=False)
    sent = lax.dynamic_index_in_dim(pieces, 1 - mine, 0, keepdims=False).astype(BF16)
    return kept, [sent]


def split_samples(kept, sent):
    total = joined(kept, sent, "rows", 0)
    dp = lax.axis_size("dp")
    channels = total.shape[-1]
    turned = total.reshape(-1, channels).T
    return shared(turned.reshape(dp, channels // dp, turned.shape[1]), "dp", 0)


def split_rows(total):
    outer = lax.axis_size("rows") // 2
    pieces = jnp.moveaxis(total.reshape(total.shape[0], outer, -1), 1, 0)
    return shared(pieces, "rows", 1)


def on_device(inputs, cotangent, weight_one, weight_two):
    picture, upstream = inputs[0], cotangent[0]
    rows, cols, channels = picture.shape
    group = lax.axis_size("rows")
    spacing = 2 * group
    factor = 1.0 / math.sqrt(lax.axis_size("dp") * rows * group * cols)
    flops = 2 * rows * cols * weight_one.shape[0] * channels
    tile = 16
    steps = rows // tile
    map_shape = jax.ShapeDtypeStruct((rows, cols, channels), BF16)
    map_spec = pl.BlockSpec((tile, cols, channels), lambda i: (i, 0, 0))
    grad_shape = jax.ShapeDtypeStruct(weight_one.shape, F32)
    grad_spec = pl.BlockSpec((3 * channels, channels), lambda a: (a, 0))
    padded = pltpu.VMEM((rows + 2 * spacing, cols + 2 * spacing, channels), BF16)
    shifted = pltpu.VMEM((3, rows + 2 * NEAR, cols, channels), BF16)
    turned = pltpu.VMEM((channels, rows * cols), BF16)
    matrix = pltpu.VMEM(weight_one.shape[::-1], BF16)

    near_low, near_high = edge_rows(picture, NEAR)
    far_low, far_high = edge_rows(upstream, spacing)
    near = (near_low, picture, near_high)
    far = (far_low, upstream, far_high)

    hidden = run(
        functools.partial(near_kernel, tile),
        map_shape, steps, map_spec, [shifted, matrix],
        (*near, weight_one), [None] * 4, flops,
    )
    hidden_low, hidden_high = edge_rows(hidden, spacing)
    grad_two = run(
        functools.partial(far_grad_kernel, spacing),
        grad_shape, 3, grad_spec, [padded, turned],
        (*far, hidden), [None] * 4, flops,
    )
    pair_two = split_pair(grad_two)
    masked = run(
        functools.partial(back_kernel, tile, spacing),
        map_shape, steps, map_spec, [padded, matrix],
        (*far, weight_two, hidden), [None] * 4 + [map_spec], flops, pair_two[1],
    )
    samples_two = split_samples(*pair_two)
    grad_one = run(
        near_grad_kernel,
        grad_shape, 3, grad_spec, [shifted, turned],
        (*near, masked), [None] * 4, flops, samples_two[1],
    )
    pair_one = split_pair(grad_one)
    early = max(1, steps // 4)
    output = run(
        functools.partial(output_kernel, tile, spacing, 0),
        map_shape, early, map_spec, [padded, matrix],
        (hidden_low, hidden, hidden_high, weight_two), [None] * 4,
        flops * early // steps, pair_one[1],
    )
    kept_one, kept_two, output = lax.optimization_barrier((pair_one[0], samples_two[0], output))
    samples_one = split_samples(kept_one, pair_one[1])
    rows_two = split_rows(joined(kept_two, samples_two[1], "dp", 0))
    if early < steps:
        output = run(
            functools.partial(output_kernel, tile, spacing, early),
            map_shape, steps - early,
            pl.BlockSpec((tile, cols, channels), lambda i: (i + early, 0, 0)), [padded, matrix],
            (hidden_low, hidden, hidden_high, weight_two), [None] * 4,
            flops * (steps - early) // steps, [output] + samples_one[1] + rows_two[1], {4: 0},
        )
    kept_one, kept_two, output = lax.optimization_barrier((samples_one[0], rows_two[0], output))
    rows_one = split_rows(joined(kept_one, samples_one[1], "dp", 0))
    grad_two = joined(kept_two, rows_two[1], "rows", 1).T
    grad_one = joined(*rows_one, "rows", 1).T
    return (output[None], grad_one * factor, grad_two * factor)


def solution(mesh):
    return jax.shard_map(
        on_device,
        mesh=mesh,
        in_specs=(P("dp", "rows", None, None), P("dp", "rows", None, None), P(), P()),
        out_specs=(P("dp", "rows", None, None), P("rows", "dp"), P("rows", "dp")),
        check_vma=False,
    )
```
